32 devices in a mesh: query: 4 (over y, x), tok: 8 (over z, core).
Axes of the slice: x: 2, y: 2, z: 4, core: 2. Of those that a mesh axis runs over, the one named last changes fastest.
Arguments:
- queries: bfloat16 [16384, 128], P('query'), may hold values from -16 to 16, as said below
- documents: bfloat16 [16384, 128], P('tok'), may hold values from -10 to 10, as said below
- cotangent: float32 [512], P('query'), may hold values from -6 to 6
Outputs:
- grad_queries: float32 [16384, 128], P(('query', 'tok'))
- grad_documents: float32 [8, 2048, 128], P('tok', 'query')
The draws below stay inside these ranges and needn't reach their ends.
Inputs may be any that keep to these rules, and one draw needn't show every extreme that they name: `documents`: document embeddings of order one. `queries`: query embeddings of order one.
All inputs are finite; a program needn't handle non-finite values.
Results may differ from the reference program's by a relative error of at most 0.0029.
Values may be sent and summed in bfloat16 or wider, within the bound.
No kernel may reach another device: no remote copies, remote signals or barrier semaphores. Data moves between devices by JAX's collectives and lax.ppermute only.
A program may use at most 64 MiB of HBM per device.

```python
import jax
import jax.numpy as jnp
from jax import lax

DIM = 128
QLEN = 32
DOC_DEV = 2048
QTOKENS = 16384
NQ = 512
NDOC = 16384
N_TOK = 8


def doc_matrix(key):
    normal_key = jax.random.fold_in(key, 11)
    values = jax.random.normal(normal_key, (NDOC, DIM), jnp.float32)
    trend = 1.0 + 0.3 * jnp.arange(NDOC).astype(jnp.float32) / NDOC
    scale = 0.3 * trend
    return jnp.clip(values * scale[:, None], -10.0, 10.0)


def draw_documents(key, part):
    return doc_matrix(key).astype(jnp.bfloat16)


def draw_queries(key, part):
    value_key = jax.random.fold_in(key, 21)
    result = jnp.clip(0.35 * jax.random.normal(value_key, (QTOKENS, DIM), jnp.float32), -8.0, 8.0)
    return result.astype(jnp.bfloat16)


def block_scale(stream_key, dims, cuts, smallest, high):
    def one(axis_at, shards_of):
        draws = jax.random.uniform(jax.random.fold_in(jax.random.fold_in(stream_key, 6), axis_at), (shards_of,), jnp.float32, smallest / len(cuts), high / len(cuts))
        return jnp.repeat(jnp.exp(draws), dims[axis_at] // shards_of).reshape((-1,) + (1,) * (len(dims) - axis_at - 1))

    level = one(*cuts[0])
    for cut in cuts[1:]:
        level = level * one(*cut)
    return level


def centred(key, shape, width, reach, cuts=(), kind=jnp.bfloat16):
    entries = jax.random.normal(key, shape, jnp.float32) * width
    if len(cuts) > 0:
        entries = block_scale(key, shape, cuts, -0.22, 0.18) * entries
    return jnp.clip(entries, min=-reach, max=reach).astype(kind)


def setup_inputs(seed: int = 0) -> dict:
    key_of = jax.random.split(jax.random.key(seed), 4)
    return {
        "queries": draw_queries(jax.random.fold_in(key_of[3], 71), 0),
        "documents": draw_documents(jax.random.fold_in(key_of[3], 71), 0),
        "cotangent": centred(key_of[2], (NQ,), 1.0, 6.0, ((0, 4),), jnp.float32),
    }


inv_temp = 2.0


def reference(queries, documents, cotangent):
    blk_rows = min(512, QTOKENS)
    n_blocks = QTOKENS // blk_rows
    row_weight = jnp.broadcast_to(cotangent[:, None], (NQ, QLEN)).reshape(-1)
    q_blocks = queries.reshape(n_blocks, blk_rows, DIM)
    weight_blocks = row_weight.reshape(n_blocks, blk_rows)

    def one_block(doc_total, inputs_blk):
        q_rows, weight_rows = inputs_blk
        scores = jnp.dot(q_rows, documents.T, preferred_element_type=jnp.float32) * inv_temp
        row_top = jnp.max(scores, axis=1)
        log_total = row_top + jnp.log(jnp.sum(jnp.exp(scores - row_top[:, None]), axis=1))
        probs = jnp.exp(scores - log_total[:, None])
        weights_low = probs.astype(jnp.bfloat16)
        grad_rows = weight_rows[:, None] * jnp.dot(weights_low, documents, preferred_element_type=jnp.float32)
        scaled = (weight_rows[:, None] * probs).astype(jnp.bfloat16)
        doc_total = doc_total + jnp.dot(scaled.T, q_rows, preferred_element_type=jnp.float32)
        return doc_total, grad_rows

    doc_total, grad_blocks = lax.scan(one_block, jnp.zeros((NDOC, DIM), jnp.float32), (q_blocks, weight_blocks))
    return grad_blocks.reshape(QTOKENS, DIM), doc_total.reshape(N_TOK, DOC_DEV, DIM)
```

```python
import functools

import jax
import jax.numpy as jnp
from jax import lax
from jax.experimental import pallas as pl
from jax.experimental.pallas import tpu as pltpu
from jax.sharding import PartitionSpec as P

QLEN = 32
SCALE = 2.0 * 1.4426950408889634
ROOM = 30.0
F32 = jnp.float32
BF16 = jnp.bfloat16


def nt_dot(a, b):
    return lax.dot_general(a, b, (((1,), (1,)), ((), ())), preferred_element_type=F32)


def nn_dot(a, b):
    return lax.dot_general(a, b, (((1,), (0,)), ((), ())), preferred_element_type=F32)


def logsum2(terms):
    top = functools.reduce(jnp.maximum, terms)
    return top + jnp.log2(sum(jnp.exp2(t - top) for t in terms))


def tile_kernel(place, q_ref, d_ref, e_ref, qt_ref, even_ref, odd_ref, lse_ref, top_ref, dt_ref, s_ref):
    nb, nd, blk = e_ref.shape
    width = d_ref.shape[1]
    step = min(256, nd)
    me = place[0]
    dt_ref[:width, :] = d_ref[...].T
    extra = (dt_ref.shape[0] - width, nd)
    dt_ref[width:, :] = jnp.where(lax.broadcasted_iota(jnp.int32, extra, 0) == 0, 1.0, 0.0).astype(BF16)

    def rows_of(p):
        return q_ref[pl.ds(pl.multiple_of((me ^ p) * blk, blk), blk), :]

    def column_max(s):
        return jnp.max(jnp.max(s.reshape(step // 8, 8, blk), axis=0), axis=0, keepdims=True)

    def finish(p, top):
        total = nn_dot(dt_ref[...], e_ref[p])
        mass = total[width : width + 1, :]
        mean = total[:width, :] * (1.0 / mass)
        half = p // 2

        @pl.when(p % 2 == 0)
        def _():
            even_ref[half] = mean

        @pl.when(p % 2 == 1)
        def _():
            odd_ref[half] = mean

        lse_ref[p] = top + jnp.log2(mass)
        top_ref[p] = top

    def quick(p, carry):
        rows = rows_of(p)
        qt_ref[p] = rows.T
        top = column_max(nt_dot(d_ref[:step, :], rows)) * SCALE
        for at in range(0, nd, step):
            s = nt_dot(d_ref[at : at + step, :], rows)
            e_ref[p, at : at + step, :] = jnp.exp2(s * SCALE - top).astype(BF16)
        finish(p, top)
        return jnp.maximum(carry, lse_ref[p] - top)

    spread = lax.fori_loop(0, nb, quick, jnp.zeros((1, blk), F32))

    @pl.when(jnp.logical_not(jnp.max(spread) <= ROOM))
    def _():
        def careful(p, carry):
            rows = rows_of(p)
            top = None
            for at in range(0, nd, step):
                s = nt_dot(d_ref[at : at + step, :], rows)
                s_ref[at : at + step, :] = s
                here = column_max(s)
                top = here if top is None else jnp.maximum(top, here)
            top = top * SCALE
            for at in range(0, nd, step):
                e_ref[p, at : at + step, :] = jnp.exp2(s_ref[at : at + step, :] * SCALE - top).astype(BF16)
            finish(p, top)
            return carry

        lax.fori_loop(0, nb, careful, 0)


def pair_kernel(even_ref, other_ref, lse_ref, other_lse_ref, pair_ref, own_ref, *send_refs):
    nb = lse_ref.shape[0]
    for p in range(nb):
        mine, theirs = lse_ref[p], other_lse_ref[p ^ 1]
        both = logsum2([mine, theirs])
        pair_ref[p] = both
        if p % 2 == 0:
            k = p // 2
            mean = even_ref[k] * jnp.exp2(mine - both) + other_ref[k] * jnp.exp2(theirs - both)
            if k == 0:
                own_ref[...] = mean
            else:
                send_refs[k - 1][...] = mean.astype(BF16)


def docs_kernel(groups, place, e_ref, qt_ref, top_ref, weight_ref, pair_ref, *refs):
    far = refs[: groups - 1]
    share_ref, own_ref = refs[groups - 1 : groups + 1]
    send_refs, fq_ref = refs[groups + 1 : -1], refs[-1]
    nb, nd, blk = e_ref.shape
    width = qt_ref.shape[1]
    me, row = place[0], place[1]
    for p in range(nb):
        parts = [pair_ref[p]] + [far[k - 1][p ^ (2 * k)] for k in range(1, groups)]
        whole = logsum2(parts)
        weight = weight_ref[me ^ p]
        if p == 0:
            for k in range(groups):
                lse_k = pair_ref[0] if k == 0 else far[k - 1][2 * k]
                share_ref[k] = weight * jnp.exp2(lse_k - whole)
        scaled = qt_ref[p].astype(F32) * (weight * jnp.exp2(top_ref[p] - whole))
        high = scaled.astype(BF16)
        fq_ref[p, :width, :] = high
        fq_ref[p, width:, :] = (scaled - high.astype(F32)).astype(BF16)
    sub = own_ref.shape[0]
    for j in range(nd // sub):
        at = pl.multiple_of((row ^ j) * sub, sub)
        total = sum(nt_dot(e_ref[p, pl.ds(at, sub), :], fq_ref[p]) for p in range(nb))
        total = total[:, :width] + total[:, width:]
        if j == 0:
            own_ref[...] = total
        else:
            send_refs[j - 1][...] = total.astype(BF16)


def query_kernel(share_ref, own_ref, *refs):
    total = share_ref[0] * own_ref[...]
    for k, ref in enumerate(refs[:-1]):
        total += share_ref[k + 1] * ref[...].astype(F32)
    refs[-1][...] = total.T


def call(kernel, name, outs, args, scalars=0, scratch=(), limit=24 << 20):
    whole = pl.BlockSpec(memory_space=pltpu.VMEM)
    scalar = pl.BlockSpec(memory_space=pltpu.SMEM)
    return pl.pallas_call(
        kernel,
        out_shape=tuple(outs),
        in_specs=[scalar] * scalars + [whole] * (len(args) - scalars),
        out_specs=(whole,) * len(outs),
        scratch_shapes=list(scratch),
        compiler_params=pltpu.CompilerParams(vmem_limit_bytes=limit),
        name=name,
    )(*args)


def swap(x, axis, step):
    return lax.ppermute(x, axis, [(i, i ^ step) for i in range(lax.axis_size(axis))])


def shards(queries, documents, cotangent):
    n, width = queries.shape
    nd = documents.shape[0]
    nb, n_row = lax.axis_size("tok"), lax.axis_size("query")
    blk, sub, groups = n // nb, nd // n_row, nb // 2
    place = jnp.stack([lax.axis_index("tok"), lax.axis_index("query")]).astype(jnp.int32)
    weights = jnp.broadcast_to(cotangent[:, None], (cotangent.shape[0], QLEN)).reshape(nb, 1, blk)
    sds = jax.ShapeDtypeStruct
    stat = sds((nb, 1, blk), F32)
    half = sds((groups, width, blk), F32)

    e, qt, even, odd, lse, top = call(
        tile_kernel,
        "tile",
        (pltpu.VMEM((nb, nd, blk), BF16), pltpu.VMEM((nb, width, blk), BF16), half, half, stat, stat),
        (place, queries, documents),
        scalars=1,
        scratch=(pltpu.VMEM((width + 16, nd), BF16), pltpu.VMEM((nd, blk), F32)),
    )
    other_lse, other = swap(lse, "tok", 1), swap(odd, "tok", 1)
    pair, own_q, *send_q = call(
        pair_kernel,
        "pair",
        (stat, sds((width, blk), F32)) + (sds((width, blk), BF16),) * (groups - 1),
        (even, other, lse, other_lse),
    )
    far = [swap(pair, "tok", 2 * k) for k in range(1, groups)]
    got_q = [swap(x, "tok", 2 * (k + 1)) for k, x in enumerate(send_q)]
    share, own_d, *send_d = call(
        functools.partial(docs_kernel, groups),
        "docs",
        (sds((groups, 1, blk), F32), sds((sub, width), F32)) + (sds((sub, width), BF16),) * (n_row - 1),
        (
            place,
            pltpu.with_memory_space_constraint(e, pltpu.VMEM),
            pltpu.with_memory_space_constraint(qt, pltpu.VMEM),
            top,
            weights,
            pair,
            *far,
        ),
        scalars=1,
        scratch=(pltpu.VMEM((nb, 2 * width, blk), BF16),),
    )
    got_d = [swap(x, "query", j + 1) for j, x in enumerate(send_d)]
    (grad_q,) = call(query_kernel, "queries", (sds((blk, width), F32),), (share, own_q, *got_q))
    grad_d = own_d
    for x in got_d:
        grad_d = grad_d + x.astype(F32)
    return grad_q, grad_d[None]


def solution(mesh):
    placed = (P("query", None), P("tok", None), P("query"))
    return jax.shard_map(
        shards,
        mesh=mesh,
        in_specs=placed,
        out_specs=(P(("query", "tok"), None), P("tok", "query", None)),
        check_vma=False,
    )
```

```python
import functools

import jax
import jax.numpy as jnp
from jax import lax
from jax.experimental import pallas as pl
from jax.experimental.pallas import tpu as pltpu
from jax.sharding import PartitionSpec as P

QLEN = 32
SCALE = 2.0 * 1.4426950408889634
ROOM = 30.0
COLUMNS = 1024
DOCS = 512
SAMPLE = 128
F32 = jnp.float32
BF16 = jnp.bfloat16
VMEM = pltpu.VMEM


def nt_dot(a, b):
    return lax.dot_general(a, b, (((1,), (1,)), ((), ())), preferred_element_type=F32)


def nn_dot(a, b):
    return lax.dot_general(a, b, (((1,), (0,)), ((), ())), preferred_element_type=F32)


def logsum2(terms):
    top = functools.reduce(jnp.maximum, terms)
    return top + jnp.log2(sum(jnp.exp2(t - top) for t in terms))


def column_max(s):
    rows, cols = s.shape
    return jnp.max(jnp.max(s.reshape(rows // 8, 8, cols), axis=0), axis=0, keepdims=True)


def tile_kernel(
    cot_ref, q_hbm, d_hbm, e_ref, qt_ref, weight_ref, even_ref, odd_ref, lse_ref, top_ref, q_ref, d_ref, dt_ref, s_ref, sems
):
    groups, nd, cols = e_ref.shape
    n, width = q_ref.shape
    nb = lax.axis_size("tok")
    me = lax.axis_index("tok")
    blk, half = n // nb, nb // 2
    step = min(DOCS, nd)
    sample = min(SAMPLE, nd)

    def block_of(slot):
        return me ^ jnp.where(slot < half, 2 * slot + 1, 2 * (slot - half))

    copies = [pltpu.make_async_copy(d_hbm, d_ref, sems.at[nb])]
    for slot in range(nb):
        source = q_hbm.at[pl.ds(pl.multiple_of(block_of(slot) * blk, blk), blk), :]
        copies.append(pltpu.make_async_copy(source, q_ref.at[slot * blk : (slot + 1) * blk, :], sems.at[slot]))
    for copy in copies:
        copy.start()

    query = lax.broadcasted_iota(jnp.int32, (1, blk), 1) // QLEN
    for slot in range(nb):
        first = block_of(slot) * (blk // QLEN)
        row = jnp.zeros((1, blk), F32)
        for at in range(blk // QLEN):
            row = jnp.where(query == at, cot_ref[first + at], row)
        group, lane = divmod(slot * blk, cols)
        weight_ref[group, :, lane : lane + blk] = row

    copies[0].wait()
    dt_ref[:width, :] = d_ref[...].T
    extra = (dt_ref.shape[0] - width, nd)
    dt_ref[width:, :] = jnp.where(lax.broadcasted_iota(jnp.int32, extra, 0) == 0, 1.0, 0.0).astype(BF16)
    for copy in copies[1:]:
        copy.wait()

    for g in range(groups):
        rows = q_ref[g * cols : (g + 1) * cols, :]
        qt_ref[g] = rows.T
        top_ref[g] = column_max(nt_dot(d_ref[:sample, :], rows)) * SCALE

    def finish(g):
        total = nn_dot(dt_ref[...], e_ref[g])
        mass = total[width : width + 1, :]
        mean = total[:width, :] * (1.0 / mass)

        @pl.when(g < groups // 2)
        def _():
            odd_ref[g] = mean.astype(BF16)

        @pl.when(g >= groups // 2)
        def _():
            even_ref[g - groups // 2] = mean

        spread = jnp.log2(mass)
        lse_ref[g] = top_ref[g] + spread
        return spread

    def quick(g, carry):
        rows = q_ref[pl.ds(pl.multiple_of(g * cols, cols), cols), :]
        top = top_ref[g]
        for at in range(0, nd, step):
            s = nt_dot(d_ref[at : at + step, :], rows)
            e_ref[g, at : at + step, :] = jnp.exp2(s * SCALE - top).astype(BF16)
        return jnp.maximum(carry, finish(g))

    spread = lax.fori_loop(0, groups, quick, jnp.zeros((1, cols), F32))

    @pl.when(jnp.logical_not(jnp.max(spread) <= ROOM))
    def _():
        def careful(g, carry):
            rows = q_ref[pl.ds(pl.multiple_of(g * cols, cols), cols), :]
            top = None
            for at in range(0, nd, step):
                s = nt_dot(d_ref[at : at + step, :], rows)
                s_ref[at : at + step, :] = s
                here = column_max(s)
                top = here if top is None else jnp.maximum(top, here)
            top = top * SCALE
            top_ref[g] = top
            for at in range(0, nd, step):
                e_ref[g, at : at + step, :] = jnp.exp2(s_ref[at : at + step, :] * SCALE - top).astype(BF16)
            finish(g)
            return carry

        lax.fori_loop(0, groups, careful, 0)


def pair_kernel(even_ref, other_ref, lse_ref, other_lse_ref, pair_ref, own_ref, *send_refs):
    groups = lse_ref.shape[0]
    width, blk = own_ref.shape
    for g in range(groups):
        mine, theirs = lse_ref[g], other_lse_ref[(g + groups // 2) % groups]
        both = logsum2([mine, theirs])
        pair_ref[g] = both
        if g >= groups // 2:
            h = g - groups // 2
            mean = even_ref[h] * jnp.exp2(mine - both) + other_ref[h].astype(F32) * jnp.exp2(theirs - both)
            per = mean.shape[1] // blk
            for i in range(per):
                k, part = h * per + i, mean[:, i * blk : (i + 1) * blk]
                if k == 0:
                    own_ref[...] = part
                else:
                    send_refs[k - 1][...] = part.astype(BF16)


def docs_kernel(chips, e_ref, qt_ref, top_ref, weight_ref, pair_ref, *refs):
    far = refs[: chips - 1]
    share_ref, own_ref = refs[chips - 1 : chips + 1]
    send_refs, fq_ref = refs[chips + 1 : -1], refs[-1]
    groups, nd, cols = e_ref.shape
    width = qt_ref.shape[1]
    blk = share_ref.shape[2]
    row = lax.axis_index("query")

    def slot_of(ref, slot):
        group, lane = divmod(slot * blk, cols)
        return ref[group, :, lane : lane + blk]

    for slot in range(groups * cols // blk):
        base, k = divmod(slot, chips)
        base *= chips
        parts = [slot_of(pair_ref, slot)] + [slot_of(far[z - 1], base + (k ^ z)) for z in range(1, chips)]
        whole = logsum2(parts)
        weight = slot_of(weight_ref, slot)
        if slot == chips:
            for z in range(chips):
                share_ref[z] = weight * jnp.exp2(parts[z] - whole)
        group, lane = divmod(slot * blk, cols)
        factor = weight * jnp.exp2(slot_of(top_ref, slot) - whole)
        scaled = qt_ref[group, :, lane : lane + blk].astype(F32) * factor
        high = scaled.astype(BF16)
        fq_ref[group, :width, lane : lane + blk] = high
        fq_ref[group, width:, lane : lane + blk] = (scaled - high.astype(F32)).astype(BF16)
    sub = own_ref.shape[0]
    for j in range(nd // sub):
        at = pl.multiple_of((row ^ j) * sub, sub)
        total = sum(nt_dot(e_ref[g, pl.ds(at, sub), :], fq_ref[g]) for g in range(groups))
        total = total[:, :width] + total[:, width:]
        if j == 0:
            own_ref[...] = total
        else:
            send_refs[j - 1][...] = total.astype(BF16)


def query_kernel(share_ref, own_ref, *refs):
    total = share_ref[0] * own_ref[...]
    for k, ref in enumerate(refs[:-1]):
        total += share_ref[k + 1] * ref[...].astype(F32)
    refs[-1][...] = total.T


def call(kernel, name, outs, args, spaces=None, scratch=(), limit=12 << 20):
    spaces = spaces or [VMEM] * len(args)
    return pl.pallas_call(
        kernel,
        out_shape=tuple(outs),
        in_specs=[pl.BlockSpec(memory_space=space) for space in spaces],
        out_specs=(pl.BlockSpec(memory_space=VMEM),) * len(outs),
        scratch_shapes=list(scratch),
        compiler_params=pltpu.CompilerParams(vmem_limit_bytes=limit),
        name=name,
    )(*args)


def swap(x, axis, step):
    return lax.ppermute(x, axis, [(i, i ^ step) for i in range(lax.axis_size(axis))])


def shards(queries, documents, cotangent):
    n, width = queries.shape
    nd = documents.shape[0]
    nb, n_row = lax.axis_size("tok"), lax.axis_size("query")
    chips = nb // 2
    blk, sub = n // nb, nd // n_row
    cols = min(max(COLUMNS, blk), n // 2)
    groups = n // cols
    sds = jax.ShapeDtypeStruct
    stat = sds((groups, 1, cols), F32)

    e, qt, weight, even, odd, lse, top = call(
        tile_kernel,
        "tile",
        (
            VMEM((groups, nd, cols), BF16),
            VMEM((groups, width, cols), BF16),
            stat,
            sds((groups // 2, width, cols), F32),
            sds((groups // 2, width, cols), BF16),
            stat,
            stat,
        ),
        (cotangent, pltpu.with_memory_space_constraint(queries, pltpu.HBM), pltpu.with_memory_space_constraint(documents, pltpu.HBM)),
        spaces=(pltpu.SMEM, pltpu.HBM, pltpu.HBM),
        scratch=(
            VMEM((n, width), BF16),
            VMEM((nd, width), BF16),
            VMEM((width + 16, nd), BF16),
            VMEM((nd, cols), F32),
            pltpu.SemaphoreType.DMA((nb + 1,)),
        ),
        limit=16 << 20,
    )
    other_lse, other = swap(lse, "tok", 1), swap(odd, "tok", 1)
    pair, own_q, *send_q = call(
        pair_kernel,
        "pair",
        (stat, sds((width, blk), F32)) + (sds((width, blk), BF16),) * (chips - 1),
        (even, other, lse, other_lse),
    )
    far = [swap(pair, "tok", 2 * k) for k in range(1, chips)]
    got_q = [swap(x, "tok", 2 * (k + 1)) for k, x in enumerate(send_q)]
    share, own_d, *send_d = call(
        functools.partial(docs_kernel, chips),
        "docs",
        (sds((chips, 1, blk), F32), sds((sub, width), F32)) + (sds((sub, width), BF16),) * (n_row - 1),
        (
            pltpu.with_memory_space_constraint(e, VMEM),
            pltpu.with_memory_space_constraint(qt, VMEM),
            top,
            weight,
            pair,
            *far,
        ),
        scratch=(VMEM((groups, 2 * width, cols), BF16),),
    )
    got_d = [swap(x, "query", j + 1) for j, x in enumerate(send_d)]
    (grad_q,) = call(query_kernel, "queries", (sds((blk, width), F32),), (share, own_q, *got_q))
    grad_d = own_d
    for x in got_d:
        grad_d = grad_d + x.astype(F32)
    return grad_q, grad_d[None]


def solution(mesh):
    placed = (P("query", None), P("tok", None), P("query"))
    return jax.shard_map(
        shards,
        mesh=mesh,
        in_specs=placed,
        out_specs=(P(("query", "tok"), None), P("tok", "query", None)),
        check_vma=False,
    )
```

```python
import functools

import jax
import jax.numpy as jnp
from jax import lax
from jax.experimental import pallas as pl
from jax.experimental.pallas import tpu as pltpu
from jax.sharding import PartitionSpec as P

QLEN = 32
SCALE = 2.0 * 1.4426950408889634
ROOM = 30.0
COLUMNS = 1024
DOCS = 512
SAMPLE = 128
F32 = jnp.float32
BF16 = jnp.bfloat16
VMEM = pltpu.VMEM


def nt_dot(a, b):
    return lax.dot_general(a, b, (((1,), (1,)), ((), ())), preferred_element_type=F32)


def nn_dot(a, b):
    return lax.dot_general(a, b, (((1,), (0,)), ((), ())), preferred_element_type=F32)


def logsum2(terms):
    top = functools.reduce(jnp.maximum, terms)
    return top + jnp.log2(sum(jnp.exp2(t - top) for t in terms))


def column_max(s):
    rows, cols = s.shape
    return jnp.max(jnp.max(s.reshape(rows // 8, 8, cols), axis=0), axis=0, keepdims=True)


def tile_kernel(
    cot_hbm, q_hbm, d_hbm, e_ref, qt_ref, weight_ref, even_ref, odd_ref, lse_ref, top_ref, cot_ref, q_ref, d_ref, dt_ref, s_ref, sems
):
    groups, nd, cols = e_ref.shape
    n, width = q_ref.shape
    nb = lax.axis_size("tok")
    me = lax.axis_index("tok")
    blk, half = n // nb, nb // 2
    step = min(DOCS, nd)
    sample = min(SAMPLE, nd)

    def block_of(slot):
        return me ^ jnp.where(slot < half, 2 * slot + 1, 2 * (slot - half))

    copies = [pltpu.make_async_copy(d_hbm, d_ref, sems.at[nb])]
    for slot in range(nb):
        source = q_hbm.at[pl.ds(pl.multiple_of(block_of(slot) * blk, blk), blk), :]
        copies.append(pltpu.make_async_copy(source, q_ref.at[slot * blk : (slot + 1) * blk, :], sems.at[slot]))
    copies.append(pltpu.make_async_copy(cot_hbm, cot_ref, sems.at[nb + 1]))
    for copy in copies:
        copy.start()
    for copy in copies:
        copy.wait()

    query = lax.broadcasted_iota(jnp.int32, (1, blk), 1) // QLEN
    for slot in range(nb):
        first = block_of(slot) * (blk // QLEN)
        row = jnp.zeros((1, blk), F32)
        for at in range(blk // QLEN):
            row = jnp.where(query == at, cot_ref[first + at], row)
        group, lane = divmod(slot * blk, cols)
        weight_ref[group, :, lane : lane + blk] = row

    dt_ref[:width, :] = d_ref[...].T
    extra = (dt_ref.shape[0] - width, nd)
    dt_ref[width:, :] = jnp.where(lax.broadcasted_iota(jnp.int32, extra, 0) == 0, 1.0, 0.0).astype(BF16)

    for g in range(groups):
        rows = q_ref[g * cols : (g + 1) * cols, :]
        qt_ref[g] = rows.T
        top_ref[g] = column_max(nt_dot(d_ref[:sample, :], rows)) * SCALE

    def finish(g):
        total = nn_dot(dt_ref[...], e_ref[g])
        mass = total[width : width + 1, :]
        mean = total[:width, :] * (1.0 / mass)

        @pl.when(g < groups // 2)
        def _():
            odd_ref[g] = mean.astype(BF16)

        @pl.when(g >= groups // 2)
        def _():
            even_ref[g - groups // 2] = mean

        spread = jnp.log2(mass)
        lse_ref[g] = top_ref[g] + spread
        return spread

    def quick(g, carry):
        rows = q_ref[pl.ds(pl.multiple_of(g * cols, cols), cols), :]
        top = top_ref[g]
        for at in range(0, nd, step):
            s = nt_dot(d_ref[at : at + step, :], rows)
            e_ref[g, at : at + step, :] = jnp.exp2(s * SCALE - top).astype(BF16)
        return jnp.maximum(carry, finish(g))

    spread = lax.fori_loop(0, groups, quick, jnp.zeros((1, cols), F32))

    @pl.when(jnp.logical_not(jnp.max(spread) <= ROOM))
    def _():
        def careful(g, carry):
            rows = q_ref[pl.ds(pl.multiple_of(g * cols, cols), cols), :]
            top = None
            for at in range(0, nd, step):
                s = nt_dot(d_ref[at : at + step, :], rows)
                s_ref[at : at + step, :] = s
                here = column_max(s)
                top = here if top is None else jnp.maximum(top, here)
            top = top * SCALE
            top_ref[g] = top
            for at in range(0, nd, step):
                e_ref[g, at : at + step, :] = jnp.exp2(s_ref[at : at + step, :] * SCALE - top).astype(BF16)
            finish(g)
            return carry

        lax.fori_loop(0, groups, careful, 0)


def pair_kernel(lse_ref, other_lse_ref, pair_ref):
    groups = lse_ref.shape[0]
    for g in range(groups):
        pair_ref[g] = logsum2([lse_ref[g], other_lse_ref[(g + groups // 2) % groups]])


def mean_kernel(even_ref, other_ref, lse_ref, other_lse_ref, pair_ref, own_ref, *send_refs):
    width, blk = own_ref.shape
    first = lse_ref.shape[0] // 2
    for h in range(first):
        both = pair_ref[first + h]
        mine, theirs = jnp.exp2(lse_ref[first + h] - both), jnp.exp2(other_lse_ref[h] - both)
        mean = even_ref[h] * mine + other_ref[h].astype(F32) * theirs
        per = mean.shape[1] // blk
        for i in range(per):
            k, part = h * per + i, mean[:, i * blk : (i + 1) * blk]
            if k == 0:
                own_ref[...] = part
            else:
                send_refs[k - 1][...] = part.astype(BF16)


def docs_kernel(chips, e_ref, qt_ref, top_ref, weight_ref, gate_ref, pair_ref, *refs):
    del gate_ref
    far = refs[: chips - 1]
    share_ref, fq_ref = refs[chips - 1 : chips + 1]
    send_refs = refs[chips + 1 :]
    groups, nd, cols = e_ref.shape
    width = qt_ref.shape[1]
    blk = share_ref.shape[2]
    row = lax.axis_index("query")

    def slot_of(ref, slot):
        group, lane = divmod(slot * blk, cols)
        return ref[group, :, lane : lane + blk]

    for slot in range(groups * cols // blk):
        base, k = divmod(slot, chips)
        base *= chips
        parts = [slot_of(pair_ref, slot)] + [slot_of(far[z - 1], base + (k ^ z)) for z in range(1, chips)]
        whole = logsum2(parts)
        weight = slot_of(weight_ref, slot)
        if slot == chips:
            for z in range(chips):
                share_ref[z] = weight * jnp.exp2(parts[z] - whole)
        group, lane = divmod(slot * blk, cols)
        factor = weight * jnp.exp2(slot_of(top_ref, slot) - whole)
        scaled = qt_ref[group, :, lane : lane + blk].astype(F32) * factor
        high = scaled.astype(BF16)
        fq_ref[group, :width, lane : lane + blk] = high
        fq_ref[group, width:, lane : lane + blk] = (scaled - high.astype(F32)).astype(BF16)
    for j, ref in enumerate(send_refs):
        ref[...] = docs_rows(e_ref, fq_ref, row ^ (j + 1), ref.shape[0]).astype(BF16)


def docs_rows(e_ref, fq_ref, at, rows):
    span = pl.ds(pl.multiple_of(at * rows, rows), rows)
    total = sum(nt_dot(e_ref[g, span, :], fq_ref[g]) for g in range(e_ref.shape[0]))
    width = total.shape[1] // 2
    return total[:, :width] + total[:, width:]


def own_docs_kernel(e_ref, fq_ref, own_ref):
    own_ref[...] = docs_rows(e_ref, fq_ref, lax.axis_index("query"), own_ref.shape[0])


def query_kernel(share_ref, own_ref, *refs):
    total = share_ref[0] * own_ref[...]
    for k, ref in enumerate(refs[:-1]):
        total += share_ref[k + 1] * ref[...].astype(F32)
    refs[-1][...] = total.T


def call(kernel, name, outs, args, spaces=None, scratch=(), limit=12 << 20, cost=None):
    spaces = spaces or [VMEM] * len(args)
    return pl.pallas_call(
        kernel,
        out_shape=tuple(outs),
        in_specs=[pl.BlockSpec(memory_space=space) for space in spaces],
        out_specs=(pl.BlockSpec(memory_space=VMEM),) * len(outs),
        scratch_shapes=list(scratch),
        compiler_params=pltpu.CompilerParams(vmem_limit_bytes=limit),
        name=name,
        cost_estimate=cost,
    )(*args)


def swap(x, axis, step):
    return lax.ppermute(x, axis, [(i, i ^ step) for i in range(lax.axis_size(axis))])


def shards(queries, documents, cotangent):
    n, width = queries.shape
    nd = documents.shape[0]
    nb, n_row = lax.axis_size("tok"), lax.axis_size("query")
    chips = nb // 2
    blk, sub = n // nb, nd // n_row
    cols = min(max(COLUMNS, blk), n // 2)
    groups = n // cols
    sds = jax.ShapeDtypeStruct
    stat = sds((groups, 1, cols), F32)

    e, qt, weight, even, odd, lse, top = call(
        tile_kernel,
        "tile",
        (
            VMEM((groups, nd, cols), BF16),
            VMEM((groups, width, cols), BF16),
            stat,
            sds((groups // 2, width, cols), F32),
            sds((groups // 2, width, cols), BF16),
            stat,
            stat,
        ),
        [pltpu.with_memory_space_constraint(x, pltpu.HBM) for x in (cotangent, queries, documents)],
        spaces=(pltpu.HBM,) * 3,
        scratch=(
            pltpu.SMEM(cotangent.shape, F32),
            VMEM((n, width), BF16),
            VMEM((nd, width), BF16),
            VMEM((width + 16, nd), BF16),
            VMEM((nd, cols), F32),
            pltpu.SemaphoreType.DMA((nb + 2,)),
        ),
        limit=16 << 20,
    )
    other_lse, other = swap(lse, "tok", 1), swap(odd, "tok", 1)
    (pair,) = call(pair_kernel, "pair", (stat,), (lse, other_lse))
    far = [swap(pair, "tok", 2 * k) for k in range(1, chips)]
    own_q, *send_q = call(
        mean_kernel,
        "mean",
        (sds((width, blk), F32),) + (sds((width, blk), BF16),) * (chips - 1),
        (even, other, lse, other_lse, pair),
    )
    got_q = [swap(x, "tok", 2 * (k + 1)) for k, x in enumerate(send_q)]
    e, qt = (pltpu.with_memory_space_constraint(x, VMEM) for x in (e, qt))
    share, fq, *send_d = call(
        functools.partial(docs_kernel, chips),
        "docs",
        (sds((chips, 1, blk), F32), VMEM((groups, 2 * width, cols), BF16)) + (sds((sub, width), BF16),) * (n_row - 1),
        (e, qt, top, weight, own_q, pair, *far),
        cost=pl.CostEstimate(flops=40 * nd * n * width, bytes_accessed=1 << 20, transcendentals=0),
    )
    got_d = [swap(x, "query", j + 1) for j, x in enumerate(send_d)]
    (own_d,) = call(
        own_docs_kernel,
        "own",
        (sds((sub, width), F32),),
        (e, pltpu.with_memory_space_constraint(fq, VMEM)),
        cost=pl.CostEstimate(flops=4 * sub * n * width, bytes_accessed=1 << 20, transcendentals=0),
    )
    (grad_q,) = call(query_kernel, "queries", (sds((blk, width), F32),), (share, own_q, *got_q))
    grad_d = own_d
    for x in got_d:
        grad_d = grad_d + x.astype(F32)
    return grad_q, grad_d[None]


def solution(mesh):
    placed = (P("query", None), P("tok", None), P("query"))
    return jax.shard_map(
        shards,
        mesh=mesh,
        in_specs=placed,
        out_specs=(P(("query", "tok"), None), P("tok", "query", None)),
        check_vma=False,
    )
```

```python
import functools

import jax
import jax.numpy as jnp
from jax import lax
from jax.experimental import pallas as pl
from jax.experimental.pallas import tpu as pltpu
from jax.sharding import PartitionSpec as P

QLEN = 32
SCALE = 2.0 * 1.4426950408889634
ROOM = 30.0
COLUMNS = 1024
DOCS = 512
SAMPLE = 128
F32 = jnp.float32
BF16 = jnp.bfloat16
VMEM = pltpu.VMEM


def nt_dot(a, b):
    return lax.dot_general(a, b, (((1,), (1,)), ((), ())), preferred_element_type=F32)


def nn_dot(a, b):
    return lax.dot_general(a, b, (((1,), (0,)), ((), ())), preferred_element_type=F32)


def logsum2(terms):
    top = functools.reduce(jnp.maximum, terms)
    return top + jnp.log2(sum(jnp.exp2(t - top) for t in terms))


def column_max(s):
    rows, cols = s.shape
    return jnp.max(jnp.max(s.reshape(rows // 8, 8, cols), axis=0), axis=0, keepdims=True)


def tile_kernel(
    cot_hbm, q_hbm, d_hbm, e_ref, qt_ref, weight_ref, even_ref, odd_ref, lse_ref, top_ref, cot_ref, q_ref, d_ref, dt_ref, s_ref, sems
):
    groups, nd, cols = e_ref.shape
    n, width = q_ref.shape
    nb = lax.axis_size("tok")
    me = lax.axis_index("tok")
    blk, half = n // nb, nb // 2
    step = min(DOCS, nd)
    sample = min(SAMPLE, nd)

    def block_of(slot):
        return me ^ jnp.where(slot < half, 2 * slot + 1, 2 * (slot - half))

    copies = [pltpu.make_async_copy(d_hbm, d_ref, sems.at[nb])]
    for slot in range(nb):
        source = q_hbm.at[pl.ds(pl.multiple_of(block_of(slot) * blk, blk), blk), :]
        copies.append(pltpu.make_async_copy(source, q_ref.at[slot * blk : (slot + 1) * blk, :], sems.at[slot]))
    copies.append(pltpu.make_async_copy(cot_hbm, cot_ref, sems.at[nb + 1]))
    for copy in copies:
        copy.start()
    copies[0].wait()
    dt_ref[:width, :] = d_ref[...].T
    extra = (dt_ref.shape[0] - width, nd)
    dt_ref[width:, :] = jnp.where(lax.broadcasted_iota(jnp.int32, extra, 0) == 0, 1.0, 0.0).astype(BF16)
    for copy in copies[1:]:
        copy.wait()

    query = lax.broadcasted_iota(jnp.int32, (1, blk), 1) // QLEN
    for slot in range(nb):
        first = block_of(slot) * (blk // QLEN)
        row = jnp.zeros((1, blk), F32)
        for at in range(blk // QLEN):
            row = jnp.where(query == at, cot_ref[first + at], row)
        group, lane = divmod(slot * blk, cols)
        weight_ref[group, :, lane : lane + blk] = row

    def finish(g, total):
        mass = total[width : width + 1, :]
        mean = total[:width, :] * (1.0 / mass)
        if g < groups // 2:
            odd_ref[g] = mean.astype(BF16)
        else:
            even_ref[g - groups // 2] = mean
        spread = jnp.log2(mass)
        lse_ref[g] = top_ref[g] + spread
        return spread

    for g in range(groups):
        top_ref[g] = column_max(nt_dot(d_ref[:sample, :], q_ref[g * cols : (g + 1) * cols, :])) * SCALE
    spread = jnp.zeros((1, cols), F32)
    for g in range(groups):
        rows = q_ref[g * cols : (g + 1) * cols, :]
        qt_ref[g] = rows.T
        top = top_ref[g]
        for at in range(0, nd, step):
            s = nt_dot(d_ref[at : at + step, :], rows)
            e_ref[g, at : at + step, :] = jnp.exp2(s * SCALE - top).astype(BF16)
        spread = jnp.maximum(spread, finish(g, nn_dot(dt_ref[...], e_ref[g])))

    @pl.when(jnp.logical_not(jnp.max(spread) <= ROOM))
    def _():
        for g in range(groups):
            rows = q_ref[g * cols : (g + 1) * cols, :]
            top = None
            for at in range(0, nd, step):
                s = nt_dot(d_ref[at : at + step, :], rows)
                s_ref[at : at + step, :] = s
                here = column_max(s)
                top = here if top is None else jnp.maximum(top, here)
            top = top * SCALE
            top_ref[g] = top
            for at in range(0, nd, step):
                e_ref[g, at : at + step, :] = jnp.exp2(s_ref[at : at + step, :] * SCALE - top).astype(BF16)
            finish(g, nn_dot(dt_ref[...], e_ref[g]))


def pair_kernel(lse_ref, other_lse_ref, pair_ref):
    groups = lse_ref.shape[0]
    for g in range(groups):
        pair_ref[g] = logsum2([lse_ref[g], other_lse_ref[(g + groups // 2) % groups]])


def mean_kernel(even_ref, other_ref, lse_ref, other_lse_ref, pair_ref, own_ref, *send_refs):
    width, blk = own_ref.shape
    first = lse_ref.shape[0] // 2
    for h in range(first):
        both = pair_ref[first + h]
        mine, theirs = jnp.exp2(lse_ref[first + h] - both), jnp.exp2(other_lse_ref[h] - both)
        mean = even_ref[h] * mine + other_ref[h].astype(F32) * theirs
        per = mean.shape[1] // blk
        for i in range(per):
            k, part = h * per + i, mean[:, i * blk : (i + 1) * blk]
            if k == 0:
                own_ref[...] = part
            else:
                send_refs[k - 1][...] = part.astype(BF16)


def docs_kernel(chips, e_ref, qt_ref, top_ref, weight_ref, gate_ref, pair_ref, *refs):
    del gate_ref
    far = refs[: chips - 1]
    share_ref, fq_ref = refs[chips - 1 : chips + 1]
    send_refs = refs[chips + 1 :]
    groups, nd, cols = e_ref.shape
    width = qt_ref.shape[1]
    blk = share_ref.shape[2]
    row = lax.axis_index("query")

    def slot_of(ref, slot):
        group, lane = divmod(slot * blk, cols)
        return ref[group, :, lane : lane + blk]

    for slot in range(groups * cols // blk):
        base, k = divmod(slot, chips)
        base *= chips
        parts = [slot_of(pair_ref, slot)] + [slot_of(far[z - 1], base + (k ^ z)) for z in range(1, chips)]
        whole = logsum2(parts)
        weight = slot_of(weight_ref, slot)
        if slot == chips:
            for z in range(chips):
                share_ref[z] = weight * jnp.exp2(parts[z] - whole)
        group, lane = divmod(slot * blk, cols)
        factor = weight * jnp.exp2(slot_of(top_ref, slot) - whole)
        scaled = qt_ref[group, :, lane : lane + blk].astype(F32) * factor
        high = scaled.astype(BF16)
        fq_ref[group, :width, lane : lane + blk] = high
        fq_ref[group, width:, lane : lane + blk] = (scaled - high.astype(F32)).astype(BF16)
    for j, ref in enumerate(send_refs):
        ref[...] = docs_rows(e_ref, fq_ref, row ^ (j + 1), ref.shape[0]).astype(BF16)


def docs_rows(e_ref, fq_ref, at, rows):
    span = pl.ds(pl.multiple_of(at * rows, rows), rows)
    total = sum(nt_dot(e_ref[g, span, :], fq_ref[g]) for g in range(e_ref.shape[0]))
    width = total.shape[1] // 2
    return total[:, :width] + total[:, width:]


def own_docs_kernel(e_ref, fq_ref, own_ref):
    own_ref[...] = docs_rows(e_ref, fq_ref, lax.axis_index("query"), own_ref.shape[0])


def query_kernel(share_ref, own_ref, *refs):
    total = share_ref[0] * own_ref[...]
    for k, ref in enumerate(refs[:-1]):
        total += share_ref[k + 1] * ref[...].astype(F32)
    refs[-1][...] = total.T


def call(kernel, name, outs, args, spaces=None, scratch=(), limit=12 << 20, cost=None):
    spaces = spaces or [VMEM] * len(args)
    return pl.pallas_call(
        kernel,
        out_shape=tuple(outs),
        in_specs=[pl.BlockSpec(memory_space=space) for space in spaces],
        out_specs=(pl.BlockSpec(memory_space=VMEM),) * len(outs),
        scratch_shapes=list(scratch),
        compiler_params=pltpu.CompilerParams(vmem_limit_bytes=limit),
        name=name,
        cost_estimate=cost,
    )(*args)


def swap(x, axis, step):
    return lax.ppermute(x, axis, [(i, i ^ step) for i in range(lax.axis_size(axis))])


def shards(queries, documents, cotangent):
    n, width = queries.shape
    nd = documents.shape[0]
    nb, n_row = lax.axis_size("tok"), lax.axis_size("query")
    chips = nb // 2
    blk, sub = n // nb, nd // n_row
    cols = min(max(COLUMNS, blk), n // 2)
    groups = n // cols
    sds = jax.ShapeDtypeStruct
    stat = sds((groups, 1, cols), F32)

    e, qt, weight, even, odd, lse, top = call(
        tile_kernel,
        "tile",
        (
            VMEM((groups, nd, cols), BF16),
            VMEM((groups, width, cols), BF16),
            stat,
            sds((groups // 2, width, cols), F32),
            sds((groups // 2, width, cols), BF16),
            stat,
            stat,
        ),
        [pltpu.with_memory_space_constraint(x, pltpu.HBM) for x in (cotangent, queries, documents)],
        spaces=(pltpu.HBM,) * 3,
        scratch=(
            pltpu.SMEM(cotangent.shape, F32),
            VMEM((n, width), BF16),
            VMEM((nd, width), BF16),
            VMEM((width + 16, nd), BF16),
            VMEM((nd, cols), F32),
            pltpu.SemaphoreType.DMA((nb + 2,)),
        ),
        limit=16 << 20,
    )
    other_lse, other = swap(lse, "tok", 1), swap(odd, "tok", 1)
    (pair,) = call(pair_kernel, "pair", (stat,), (lse, other_lse))
    far = [swap(pair, "tok", 2 * k) for k in range(1, chips)]
    own_q, *send_q = call(
        mean_kernel,
        "mean",
        (sds((width, blk), F32),) + (sds((width, blk), BF16),) * (chips - 1),
        (even, other, lse, other_lse, pair),
    )
    got_q = [swap(x, "tok", 2 * (k + 1)) for k, x in enumerate(send_q)]
    e, qt = (pltpu.with_memory_space_constraint(x, VMEM) for x in (e, qt))
    share, fq, *send_d = call(
        functools.partial(docs_kernel, chips),
        "docs",
        (sds((chips, 1, blk), F32), VMEM((groups, 2 * width, cols), BF16)) + (sds((sub, width), BF16),) * (n_row - 1),
        (e, qt, top, weight, own_q, pair, *far),
        cost=pl.CostEstimate(flops=40 * nd * n * width, bytes_accessed=1 << 20, transcendentals=0),
    )
    got_d = [swap(x, "query", j + 1) for j, x in enumerate(send_d)]
    (own_d,) = call(
        own_docs_kernel,
        "own",
        (sds((sub, width), F32),),
        (e, pltpu.with_memory_space_constraint(fq, VMEM)),
        cost=pl.CostEstimate(flops=4 * sub * n * width, bytes_accessed=1 << 20, transcendentals=0),
    )
    (grad_q,) = call(query_kernel, "queries", (sds((blk, width), F32),), (share, own_q, *got_q))
    grad_d = own_d
    for x in reversed(got_d):
        grad_d = grad_d + x.astype(F32)
    return grad_q, grad_d[None]


def solution(mesh):
    placed = (P("query", None), P("tok", None), P("query"))
    return jax.shard_map(
        shards,
        mesh=mesh,
        in_specs=placed,
        out_specs=(P(("query", "tok"), None), P("tok", "query", None)),
        check_vma=False,
    )
```

```python
import functools

import jax
import jax.numpy as jnp
from jax import lax
from jax.experimental import pallas as pl
from jax.experimental.pallas import tpu as pltpu
from jax.sharding import PartitionSpec as P

QLEN = 32
SCALE = 2.0 * 1.4426950408889634
ROOM = 30.0
COLUMNS = 1024
DOCS = 512
SAMPLE = 128
F32 = jnp.float32
BF16 = jnp.bfloat16
VMEM = pltpu.VMEM


def nt_dot(a, b):
    return lax.dot_general(a, b, (((1,), (1,)), ((), ())), preferred_element_type=F32)


def nn_dot(a, b):
    return lax.dot_general(a, b, (((1,), (0,)), ((), ())), preferred_element_type=F32)


def logsum2(terms):
    top = functools.reduce(jnp.maximum, terms)
    return top + jnp.log2(sum(jnp.exp2(t - top) for t in terms))


def column_max(s):
    rows, cols = s.shape
    return jnp.max(jnp.max(s.reshape(rows // 8, 8, cols), axis=0), axis=0, keepdims=True)


def tile_kernel(
    cot_hbm, q_hbm, d_hbm, e_ref, qt_ref, weight_ref, odd_ref, lse_ref, top_ref, dt_ref, cot_ref, q_ref, d_ref, s_ref, sems
):
    groups, nd, cols = e_ref.shape
    n, width = q_ref.shape
    nb = lax.axis_size("tok")
    me = lax.axis_index("tok")
    blk, half = n // nb, nb // 2
    step = min(DOCS, nd)
    sample = min(SAMPLE, nd)

    def block_of(slot):
        return me ^ jnp.where(slot < half, 2 * slot + 1, 2 * (slot - half))

    copies = [pltpu.make_async_copy(d_hbm, d_ref, sems.at[nb])]
    for slot in range(nb):
        source = q_hbm.at[pl.ds(pl.multiple_of(block_of(slot) * blk, blk), blk), :]
        copies.append(pltpu.make_async_copy(source, q_ref.at[slot * blk : (slot + 1) * blk, :], sems.at[slot]))
    copies.append(pltpu.make_async_copy(cot_hbm, cot_ref, sems.at[nb + 1]))
    for copy in copies:
        copy.start()
    copies[0].wait()
    dt_ref[:width, :] = d_ref[...].T
    extra = (dt_ref.shape[0] - width, nd)
    dt_ref[width:, :] = jnp.where(lax.broadcasted_iota(jnp.int32, extra, 0) == 0, 1.0, 0.0).astype(BF16)
    for copy in copies[1:]:
        copy.wait()

    query = lax.broadcasted_iota(jnp.int32, (1, blk), 1) // QLEN
    for slot in range(nb):
        first = block_of(slot) * (blk // QLEN)
        row = jnp.zeros((1, blk), F32)
        for at in range(blk // QLEN):
            row = jnp.where(query == at, cot_ref[first + at], row)
        group, lane = divmod(slot * blk, cols)
        weight_ref[group, :, lane : lane + blk] = row

    def finish(g, sums):
        if g < groups // 2:
            total = nn_dot(dt_ref[...], e_ref[g])
            mass = total[width : width + 1, :]
            odd_ref[g] = (total[:width, :] * (1.0 / mass)).astype(BF16)
        else:
            mass = jnp.sum(sums, axis=0, keepdims=True)
        spread = jnp.log2(mass)
        lse_ref[g] = top_ref[g] + spread
        return spread

    for g in range(groups):
        top_ref[g] = column_max(nt_dot(d_ref[:sample, :], q_ref[g * cols : (g + 1) * cols, :])) * SCALE
    spread = jnp.zeros((1, cols), F32)
    for g in range(groups):
        rows = q_ref[g * cols : (g + 1) * cols, :]
        qt_ref[g] = rows.T
        top = top_ref[g]
        sums = jnp.zeros((8, cols), F32)
        for at in range(0, nd, step):
            s = nt_dot(d_ref[at : at + step, :], rows)
            e = jnp.exp2(s * SCALE - top)
            e_ref[g, at : at + step, :] = e.astype(BF16)
            if g >= groups // 2:
                sums = sums + jnp.sum(e.reshape(step // 8, 8, cols), axis=0)
        spread = jnp.maximum(spread, finish(g, sums))

    @pl.when(jnp.logical_not(jnp.max(spread) <= ROOM))
    def _():
        for g in range(groups):
            rows = q_ref[g * cols : (g + 1) * cols, :]
            top = None
            sums = jnp.zeros((8, cols), F32)
            for at in range(0, nd, step):
                s = nt_dot(d_ref[at : at + step, :], rows)
                s_ref[at : at + step, :] = s
                here = column_max(s)
                top = here if top is None else jnp.maximum(top, here)
            top = top * SCALE
            top_ref[g] = top
            for at in range(0, nd, step):
                e = jnp.exp2(s_ref[at : at + step, :] * SCALE - top)
                e_ref[g, at : at + step, :] = e.astype(BF16)
                sums = sums + jnp.sum(e.reshape(step // 8, 8, cols), axis=0)
            finish(g, sums)


def even_kernel(e_ref, dt_ref, lse_ref, top_ref, even_ref):
    half, width, _ = even_ref.shape
    for h in range(half):
        total = nn_dot(dt_ref[:width, :], e_ref[half + h])
        even_ref[h] = total * jnp.exp2(top_ref[half + h] - lse_ref[half + h])


def pair_kernel(lse_ref, other_lse_ref, gate_ref, pair_ref):
    del gate_ref
    groups = lse_ref.shape[0]
    for g in range(groups):
        pair_ref[g] = logsum2([lse_ref[g], other_lse_ref[(g + groups // 2) % groups]])


def mean_kernel(even_ref, other_ref, lse_ref, other_lse_ref, pair_ref, own_ref, *send_refs):
    width, blk = own_ref.shape
    first = lse_ref.shape[0] // 2
    for h in range(first):
        both = pair_ref[first + h]
        mine, theirs = jnp.exp2(lse_ref[first + h] - both), jnp.exp2(other_lse_ref[h] - both)
        mean = even_ref[h] * mine + other_ref[h].astype(F32) * theirs
        per = mean.shape[1] // blk
        for i in range(per):
            k, part = h * per + i, mean[:, i * blk : (i + 1) * blk]
            if k == 0:
                own_ref[...] = part
            else:
                send_refs[k - 1][...] = part.astype(BF16)


def far_order(chips):
    return [0] + list(range(chips - 2, 0, -1))


def docs_kernel(chips, e_ref, qt_ref, top_ref, weight_ref, gate_ref, pair_ref, *refs):
    del gate_ref
    far = [ref for _, ref in sorted(zip(far_order(chips), refs), key=lambda pair: pair[0])]
    share_ref, fq_ref = refs[chips - 1 : chips + 1]
    send_refs = refs[chips + 1 :]
    groups, nd, cols = e_ref.shape
    width = qt_ref.shape[1]
    blk = share_ref.shape[2]
    row = lax.axis_index("query")

    def slot_of(ref, slot):
        group, lane = divmod(slot * blk, cols)
        return ref[group, :, lane : lane + blk]

    for slot in range(groups * cols // blk):
        base, k = divmod(slot, chips)
        base *= chips
        parts = [slot_of(pair_ref, slot)] + [slot_of(far[z - 1], base + (k ^ z)) for z in range(1, chips)]
        whole = logsum2(parts)
        weight = slot_of(weight_ref, slot)
        if slot == chips:
            for z in range(chips):
                share_ref[z] = weight * jnp.exp2(parts[z] - whole)
        group, lane = divmod(slot * blk, cols)
        factor = weight * jnp.exp2(slot_of(top_ref, slot) - whole)
        scaled = qt_ref[group, :, lane : lane + blk].astype(F32) * factor
        high = scaled.astype(BF16)
        fq_ref[group, :width, lane : lane + blk] = high
        fq_ref[group, width:, lane : lane + blk] = (scaled - high.astype(F32)).astype(BF16)
    for j, ref in enumerate(send_refs):
        ref[...] = docs_rows(e_ref, fq_ref, row ^ (j + 1), ref.shape[0]).astype(BF16)


def docs_rows(e_ref, fq_ref, at, rows):
    span = pl.ds(pl.multiple_of(at * rows, rows), rows)
    total = sum(nt_dot(e_ref[g, span, :], fq_ref[g]) for g in range(e_ref.shape[0]))
    width = total.shape[1] // 2
    return total[:, :width] + total[:, width:]


def own_docs_kernel(e_ref, fq_ref, own_ref):
    own_ref[...] = docs_rows(e_ref, fq_ref, lax.axis_index("query"), own_ref.shape[0])


def query_kernel(share_ref, own_ref, *refs):
    total = share_ref[0] * own_ref[...]
    for k, ref in enumerate(refs[:-1]):
        total += share_ref[k + 1] * ref[...].astype(F32)
    refs[-1][...] = total.T


def call(kernel, name, outs, args, spaces=None, scratch=(), limit=12 << 20, cost=None):
    spaces = spaces or [VMEM] * len(args)
    return pl.pallas_call(
        kernel,
        out_shape=tuple(outs),
        in_specs=[pl.BlockSpec(memory_space=space) for space in spaces],
        out_specs=(pl.BlockSpec(memory_space=VMEM),) * len(outs),
        scratch_shapes=list(scratch),
        compiler_params=pltpu.CompilerParams(vmem_limit_bytes=limit),
        name=name,
        cost_estimate=cost,
    )(*args)


def swap(x, axis, step):
    return lax.ppermute(x, axis, [(i, i ^ step) for i in range(lax.axis_size(axis))])


def shards(queries, documents, cotangent):
    n, width = queries.shape
    nd = documents.shape[0]
    nb, n_row = lax.axis_size("tok"), lax.axis_size("query")
    chips = nb // 2
    blk, sub = n // nb, nd // n_row
    cols = min(max(COLUMNS, blk), n // 2)
    groups = n // cols
    sds = jax.ShapeDtypeStruct
    stat = sds((groups, 1, cols), F32)

    e, qt, weight, odd, lse, top, dt = call(
        tile_kernel,
        "tile",
        (
            VMEM((groups, nd, cols), BF16),
            VMEM((groups, width, cols), BF16),
            stat,
            sds((groups // 2, width, cols), BF16),
            stat,
            stat,
            VMEM((width + 16, nd), BF16),
        ),
        [pltpu.with_memory_space_constraint(x, pltpu.HBM) for x in (cotangent, queries, documents)],
        spaces=(pltpu.HBM,) * 3,
        scratch=(
            pltpu.SMEM(cotangent.shape, F32),
            VMEM((n, width), BF16),
            VMEM((nd, width), BF16),
            VMEM((nd, cols), F32),
            pltpu.SemaphoreType.DMA((nb + 2,)),
        ),
        limit=16 << 20,
    )
    other_lse, other = swap(lse, "tok", 1), swap(odd, "tok", 1)
    e, qt, dt = (pltpu.with_memory_space_constraint(x, VMEM) for x in (e, qt, dt))
    (even,) = call(
        even_kernel,
        "even",
        (sds((groups // 2, width, cols), F32),),
        (e, dt, lse, top),
        cost=pl.CostEstimate(flops=8 * nd * n * width, bytes_accessed=1 << 20, transcendentals=0),
    )
    (pair,) = call(pair_kernel, "pair", (stat,), (lse, other_lse, even))
    far = [swap(pair, "tok", 2 * k) for k in range(1, chips)]
    own_q, *send_q = call(
        mean_kernel,
        "mean",
        (sds((width, blk), F32),) + (sds((width, blk), BF16),) * (chips - 1),
        (even, other, lse, other_lse, pair),
    )
    got_q = [swap(x, "tok", 2 * (k + 1)) for k, x in enumerate(send_q)]
    share, fq, *send_d = call(
        functools.partial(docs_kernel, chips),
        "docs",
        (sds((chips, 1, blk), F32), VMEM((groups, 2 * width, cols), BF16)) + (sds((sub, width), BF16),) * (n_row - 1),
        (e, qt, top, weight, own_q, pair, *[far[i] for i in far_order(chips)]),
        cost=pl.CostEstimate(flops=40 * nd * n * width, bytes_accessed=1 << 20, transcendentals=0),
    )
    got_d = [swap(x, "query", j + 1) for j, x in enumerate(send_d)]
    (own_d,) = call(
        own_docs_kernel,
        "own",
        (sds((sub, width), F32),),
        (e, pltpu.with_memory_space_constraint(fq, VMEM)),
        cost=pl.CostEstimate(flops=4 * sub * n * width, bytes_accessed=1 << 20, transcendentals=0),
    )
    (grad_q,) = call(query_kernel, "queries", (sds((blk, width), F32),), (share, own_q, *got_q))
    grad_d = own_d
    for x in reversed(got_d):
        grad_d = grad_d + x.astype(F32)
    return grad_q, grad_d[None]


def solution(mesh):
    placed = (P("query", None), P("tok", None), P("query"))
    return jax.shard_map(
        shards,
        mesh=mesh,
        in_specs=placed,
        out_specs=(P(("query", "tok"), None), P("tok", "query", None)),
        check_vma=False,
    )
```

```python
import functools

import jax
import jax.numpy as jnp
from jax import lax
from jax.experimental import pallas as pl
from jax.experimental.pallas import tpu as pltpu
from jax.sharding import PartitionSpec as P

QLEN = 32
SCALE = 2.0 * 1.4426950408889634
ROOM = 30.0
COLUMNS = 1024
DOCS = 1024
SAMPLE = 128
F32 = jnp.float32
BF16 = jnp.bfloat16
VMEM = pltpu.VMEM


def nt_dot(a, b):
    return lax.dot_general(a, b, (((1,), (1,)), ((), ())), preferred_element_type=F32)


def nn_dot(a, b):
    return lax.dot_general(a, b, (((1,), (0,)), ((), ())), preferred_element_type=F32)


def logsum2(terms):
    top = functools.reduce(jnp.maximum, terms)
    return top + jnp.log2(sum(jnp.exp2(t - top) for t in terms))


def column_max(s):
    rows, cols = s.shape
    return jnp.max(jnp.max(s.reshape(rows // 8, 8, cols), axis=0), axis=0, keepdims=True)


def tile_kernel(
    cot_hbm, q_hbm, d_hbm, e_ref, qt_ref, weight_ref, odd_ref, lse_ref, top_ref, dt_ref, cot_ref, q_ref, d_ref, s_ref, sems
):
    groups, nd, cols = e_ref.shape
    n, width = q_ref.shape
    nb = lax.axis_size("tok")
    me = lax.axis_index("tok")
    blk, half = n // nb, nb // 2
    step = min(DOCS, nd)
    sample = min(SAMPLE, nd)

    def block_of(slot):
        return me ^ jnp.where(slot < half, 2 * slot + 1, 2 * (slot - half))

    copies = [pltpu.make_async_copy(d_hbm, d_ref, sems.at[nb])]
    for slot in range(nb):
        source = q_hbm.at[pl.ds(pl.multiple_of(block_of(slot) * blk, blk), blk), :]
        copies.append(pltpu.make_async_copy(source, q_ref.at[slot * blk : (slot + 1) * blk, :], sems.at[slot]))
    copies.append(pltpu.make_async_copy(cot_hbm, cot_ref, sems.at[nb + 1]))
    for copy in copies:
        copy.start()
    copies[0].wait()
    dt_ref[:width, :] = d_ref[...].T
    extra = (dt_ref.shape[0] - width, nd)
    dt_ref[width:, :] = jnp.where(lax.broadcasted_iota(jnp.int32, extra, 0) == 0, 1.0, 0.0).astype(BF16)
    for copy in copies[1:]:
        copy.wait()

    query = lax.broadcasted_iota(jnp.int32, (1, blk), 1) // QLEN
    for slot in range(nb):
        first = block_of(slot) * (blk // QLEN)
        row = jnp.zeros((1, blk), F32)
        for at in range(blk // QLEN):
            row = jnp.where(query == at, cot_ref[first + at], row)
        group, lane = divmod(slot * blk, cols)
        weight_ref[group, :, lane : lane + blk] = row

    def finish(g, sums):
        if g < groups // 2:
            total = nn_dot(dt_ref[...], e_ref[g])
            mass = total[width : width + 1, :]
            odd_ref[g] = (total[:width, :] * (1.0 / mass)).astype(BF16)
        else:
            mass = jnp.sum(sums, axis=0, keepdims=True)
        spread = jnp.log2(mass)
        lse_ref[g] = top_ref[g] + spread
        return spread

    for g in range(groups):
        top_ref[g] = column_max(nt_dot(d_ref[:sample, :], q_ref[g * cols : (g + 1) * cols, :])) * SCALE
    spread = jnp.zeros((1, cols), F32)
    for g in range(groups):
        rows = q_ref[g * cols : (g + 1) * cols, :]
        qt_ref[g] = rows.T
        top = top_ref[g]
        sums = jnp.zeros((8, cols), F32)
        for at in range(0, nd, step):
            s = nt_dot(d_ref[at : at + step, :], rows)
            e = jnp.exp2(s * SCALE - top)
            e_ref[g, at : at + step, :] = e.astype(BF16)
            if g >= groups // 2:
                sums = sums + jnp.sum(e.reshape(step // 8, 8, cols), axis=0)
        spread = jnp.maximum(spread, finish(g, sums))

    @pl.when(jnp.logical_not(jnp.max(spread) <= ROOM))
    def _():
        for g in range(groups):
            rows = q_ref[g * cols : (g + 1) * cols, :]
            top = None
            sums = jnp.zeros((8, cols), F32)
            for at in range(0, nd, step):
                s = nt_dot(d_ref[at : at + step, :], rows)
                s_ref[at : at + step, :] = s
                here = column_max(s)
                top = here if top is None else jnp.maximum(top, here)
            top = top * SCALE
            top_ref[g] = top
            for at in range(0, nd, step):
                e = jnp.exp2(s_ref[at : at + step, :] * SCALE - top)
                e_ref[g, at : at + step, :] = e.astype(BF16)
                sums = sums + jnp.sum(e.reshape(step // 8, 8, cols), axis=0)
            finish(g, sums)


def even_kernel(e_ref, dt_ref, lse_ref, top_ref, even_ref):
    half, width, _ = even_ref.shape
    for h in range(half):
        total = nn_dot(dt_ref[:width, :], e_ref[half + h])
        even_ref[h] = total * jnp.exp2(top_ref[half + h] - lse_ref[half + h])


def pair_kernel(lse_ref, other_lse_ref, gate_ref, pair_ref):
    del gate_ref
    groups = lse_ref.shape[0]
    for g in range(groups):
        pair_ref[g] = logsum2([lse_ref[g], other_lse_ref[(g + groups // 2) % groups]])


def mean_kernel(even_ref, other_ref, lse_ref, other_lse_ref, pair_ref, own_ref, *send_refs):
    width, blk = own_ref.shape
    first = lse_ref.shape[0] // 2
    for h in range(first):
        both = pair_ref[first + h]
        mine, theirs = jnp.exp2(lse_ref[first + h] - both), jnp.exp2(other_lse_ref[h] - both)
        mean = even_ref[h] * mine + other_ref[h].astype(F32) * theirs
        per = mean.shape[1] // blk
        for i in range(per):
            k, part = h * per + i, mean[:, i * blk : (i + 1) * blk]
            if k == 0:
                own_ref[...] = part
            else:
                send_refs[k - 1][...] = part.astype(BF16)


def far_order(chips):
    return [0] + list(range(chips - 2, 0, -1))


def docs_kernel(chips, e_ref, qt_ref, top_ref, weight_ref, gate_ref, pair_ref, *refs):
    del gate_ref
    far = [ref for _, ref in sorted(zip(far_order(chips), refs), key=lambda pair: pair[0])]
    share_ref, fq_ref = refs[chips - 1 : chips + 1]
    send_refs = refs[chips + 1 :]
    groups, nd, cols = e_ref.shape
    width = qt_ref.shape[1]
    blk = share_ref.shape[2]
    row = lax.axis_index("query")

    def slot_of(ref, slot):
        group, lane = divmod(slot * blk, cols)
        return ref[group, :, lane : lane + blk]

    for slot in range(groups * cols // blk):
        base, k = divmod(slot, chips)
        base *= chips
        parts = [slot_of(pair_ref, slot)] + [slot_of(far[z - 1], base + (k ^ z)) for z in range(1, chips)]
        whole = logsum2(parts)
        weight = slot_of(weight_ref, slot)
        if slot == chips:
            for z in range(chips):
                share_ref[z] = weight * jnp.exp2(parts[z] - whole)
        group, lane = divmod(slot * blk, cols)
        factor = weight * jnp.exp2(slot_of(top_ref, slot) - whole)
        scaled = qt_ref[group, :, lane : lane + blk].astype(F32) * factor
        high = scaled.astype(BF16)
        fq_ref[group, :width, lane : lane + blk] = high
        fq_ref[group, width:, lane : lane + blk] = (scaled - high.astype(F32)).astype(BF16)
    for j, ref in enumerate(send_refs):
        ref[...] = docs_rows(e_ref, fq_ref, row ^ (j + 1), ref.shape[0]).astype(BF16)


def docs_rows(e_ref, fq_ref, at, rows):
    span = pl.ds(pl.multiple_of(at * rows, rows), rows)
    total = sum(nt_dot(e_ref[g, span, :], fq_ref[g]) for g in range(e_ref.shape[0]))
    width = total.shape[1] // 2
    return total[:, :width] + total[:, width:]


def own_docs_kernel(e_ref, fq_ref, own_ref):
    own_ref[...] = docs_rows(e_ref, fq_ref, lax.axis_index("query"), own_ref.shape[0])


def query_kernel(share_ref, own_ref, *refs):
    total = share_ref[0] * own_ref[...]
    for k, ref in enumerate(refs[:-1]):
        total += share_ref[k + 1] * ref[...].astype(F32)
    refs[-1][...] = total.T


def call(kernel, name, outs, args, spaces=None, scratch=(), limit=12 << 20, cost=None):
    spaces = spaces or [VMEM] * len(args)
    return pl.pallas_call(
        kernel,
        out_shape=tuple(outs),
        in_specs=[pl.BlockSpec(memory_space=space) for space in spaces],
        out_specs=(pl.BlockSpec(memory_space=VMEM),) * len(outs),
        scratch_shapes=list(scratch),
        compiler_params=pltpu.CompilerParams(vmem_limit_bytes=limit),
        name=name,
        cost_estimate=cost,
    )(*args)


def swap(x, axis, step):
    return lax.ppermute(x, axis, [(i, i ^ step) for i in range(lax.axis_size(axis))])


def shards(queries, documents, cotangent):
    n, width = queries.shape
    nd = documents.shape[0]
    nb, n_row = lax.axis_size("tok"), lax.axis_size("query")
    chips = nb // 2
    blk, sub = n // nb, nd // n_row
    cols = min(max(COLUMNS, blk), n // 2)
    groups = n // cols
    sds = jax.ShapeDtypeStruct
    stat = sds((groups, 1, cols), F32)

    e, qt, weight, odd, lse, top, dt = call(
        tile_kernel,
        "tile",
        (
            VMEM((groups, nd, cols), BF16),
            VMEM((groups, width, cols), BF16),
            stat,
            sds((groups // 2, width, cols), BF16),
            stat,
            stat,
            VMEM((width + 16, nd), BF16),
        ),
        [pltpu.with_memory_space_constraint(x, pltpu.HBM) for x in (cotangent, queries, documents)],
        spaces=(pltpu.HBM,) * 3,
        scratch=(
            pltpu.SMEM(cotangent.shape, F32),
            VMEM((n, width), BF16),
            VMEM((nd, width), BF16),
            VMEM((nd, cols), F32),
            pltpu.SemaphoreType.DMA((nb + 2,)),
        ),
        limit=16 << 20,
    )
    other_lse, other = swap(lse, "tok", 1), swap(odd, "tok", 1)
    e, qt, dt = (pltpu.with_memory_space_constraint(x, VMEM) for x in (e, qt, dt))
    (even,) = call(
        even_kernel,
        "even",
        (sds((groups // 2, width, cols), F32),),
        (e, dt, lse, top),
        cost=pl.CostEstimate(flops=8 * nd * n * width, bytes_accessed=1 << 20, transcendentals=0),
    )
    (pair,) = call(pair_kernel, "pair", (stat,), (lse, other_lse, even))
    far = [swap(pair, "tok", 2 * k) for k in range(1, chips)]
    own_q, *send_q = call(
        mean_kernel,
        "mean",
        (sds((width, blk), F32),) + (sds((width, blk), BF16),) * (chips - 1),
        (even, other, lse, other_lse, pair),
    )
    got_q = [swap(x, "tok", 2 * (k + 1)) for k, x in enumerate(send_q)]
    share, fq, *send_d = call(
        functools.partial(docs_kernel, chips),
        "docs",
        (sds((chips, 1, blk), F32), VMEM((groups, 2 * width, cols), BF16)) + (sds((sub, width), BF16),) * (n_row - 1),
        (e, qt, top, weight, own_q, pair, *[far[i] for i in far_order(chips)]),
        cost=pl.CostEstimate(flops=40 * nd * n * width, bytes_accessed=1 << 20, transcendentals=0),
    )
    got_d = [swap(x, "query", j + 1) for j, x in enumerate(send_d)]
    (own_d,) = call(
        own_docs_kernel,
        "own",
        (sds((sub, width), F32),),
        (e, pltpu.with_memory_space_constraint(fq, VMEM)),
        cost=pl.CostEstimate(flops=4 * sub * n * width, bytes_accessed=1 << 20, transcendentals=0),
    )
    (grad_q,) = call(query_kernel, "queries", (sds((blk, width), F32),), (share, own_q, *got_q))
    grad_d = own_d
    for x in reversed(got_d):
        grad_d = grad_d + x.astype(F32)
    return grad_q, grad_d[None]


def solution(mesh):
    placed = (P("query", None), P("tok", None), P("query"))
    return jax.shard_map(
        shards,
        mesh=mesh,
        in_specs=placed,
        out_specs=(P(("query", "tok"), None), P("tok", "query", None)),
        check_vma=False,
    )
```
